32 devices in a mesh: groups: 2 (over x), patch: 16 (over z, y, core).
Axes of the slice: x: 2, y: 2, z: 4, core: 2. Of those that a mesh axis runs over, the one named last changes fastest.
Arguments:
- trial: float32 [64, 262144], P('groups', 'patch'), parts along dimension 0
- loads: float32 [8, 262144], P(None, 'patch'), may hold values from -6 to 6
- band: float32 [9, 262144], P(None, 'patch'), may hold values from -3 to 3
- seeds: int32 [64], P('groups'), parts along dimension 0, may hold values from 0 to 7
- iface_rows: int32 [2048], P('patch'), may hold values from 0 to 16383, as said below
- iface_partner: int32 [2048], P('patch'), may hold values from 0 to 2047, as said below
- patch_device: int32 [16], replicated, may hold values from 0 to 15, as said below
- iface_weight: float32 [2048], P('patch'), may hold values from 0.5 to 1.5
Outputs:
- r_factor: float32 [64, 32], P('groups'), parts along dimension 0
- basis: float32 [64, 262144], P('groups', 'patch'), parts along dimension 0
The draws below stay inside these ranges and needn't reach their ends.
There are 2 independent parts, one for each index of `groups`. The reference program is written for one: setup_inputs(seed, part) draws one part's arguments, and reference() takes and returns one part's arrays. A program takes and returns all parts, laid end to end along the dimension named above; an argument that names none is the same for every part. Nothing has to cross between parts.
Inputs may be any that keep to these rules, and one draw needn't show every extreme that they name: `iface_rows`: the 128 slots of one device name distinct local unknowns, among them 0 and 16383. `iface_partner`: patches form a closed cycle in block order: with other as in the reference program, other[other[i]] = i and other[i] != i; a slot i with i % 128 < 64 is paired with a slot of block (i // 128 + 1) mod 16 whose index modulo 128 is 64 or more, so a patch shares slots with at most 2 other patches, 64 slots with each. `patch_device`: A permutation of the patches.
All inputs are finite; a program needn't handle non-finite values.
Results may differ from the reference program's by a relative error of at most 0.00005.
Values sent between devices are 32-bit elements; how exact they have to be, the bound alone decides.
A program may use at most 64 MiB of HBM per device.

```python
import math
import jax
import jax.numpy as jnp
from jax import lax

SNAP = 32
ROWS_DEV = 16384
IFACE = 128
BAND = 9
NLOAD = 8
PATCHES = 16
ROWS_ALL = 262144
SLOTS = 2048


def draw_trial(key, part):
    key = jax.random.fold_in(key, 11)
    first, second, third = jax.random.split(key, 3)
    blk = jnp.arange(ROWS_ALL) // ROWS_DEV
    rise = jnp.exp(math.log(3.0) * blk.astype(jnp.float32) / max(PATCHES - 1, 1))
    column = jnp.exp(jax.random.uniform(second, (SNAP, 1), minval=math.log(0.3), maxval=math.log(3.0)))
    rough = jnp.exp(jax.random.uniform(third, (1, ROWS_ALL), minval=math.log(0.5), maxval=math.log(2.0)))
    base = jax.random.normal(first, (SNAP, ROWS_ALL))
    return (base * column * rough * rise[None, :]).astype(jnp.float32)


def draw_iface_rows(key, part):
    key = jax.random.fold_in(key, 23)
    keys = jax.random.split(key, PATCHES)

    def one_patch(patch_key):
        pick_key, order_key = jax.random.split(patch_key)
        middle = 1 + jax.random.permutation(pick_key, ROWS_DEV - 2)[:IFACE - 2]
        rows = jnp.concatenate([jnp.array([0, ROWS_DEV - 1], jnp.int32), middle.astype(jnp.int32)])
        return rows[jax.random.permutation(order_key, IFACE)]
    return jax.vmap(one_patch)(keys).reshape(-1).astype(jnp.int32)


def cycle_layout(key):
    label_key, pair_key = jax.random.split(jax.random.fold_in(key, 41))
    label_block = jax.random.permutation(label_key, PATCHES).astype(jnp.int32)
    half_slots = IFACE // 2
    pair_keys = jax.random.split(pair_key, PATCHES)
    pairing = jax.vmap(lambda k: jax.random.permutation(k, half_slots))(pair_keys).astype(jnp.int32)
    return (label_block, pairing)


def draw_patch_device(key, part):
    label_block, pairing = cycle_layout(key)
    return label_block


def draw_iface_partner(key, part):
    label_block, pairing = cycle_layout(key)
    half_slots = IFACE // 2
    block_label = jnp.zeros((PATCHES,), jnp.int32).at[label_block].set(jnp.arange(PATCHES, dtype=jnp.int32))
    inverse = jnp.zeros((PATCHES, half_slots), jnp.int32)
    inverse = inverse.at[jnp.arange(PATCHES, dtype=jnp.int32)[:, None], pairing].set(jnp.broadcast_to(jnp.arange(half_slots, dtype=jnp.int32)[None, :], (PATCHES, half_slots)))
    blocks = jnp.arange(PATCHES, dtype=jnp.int32)
    next_block = (blocks + 1) % PATCHES
    prev_block = (blocks + PATCHES - 1) % PATCHES
    lower_part = block_label[next_block][:, None] * IFACE + half_slots + pairing
    upper_part = block_label[prev_block][:, None] * IFACE + inverse[prev_block]
    return jnp.concatenate([lower_part, upper_part], axis=1).reshape(-1).astype(jnp.int32)


def set_ends(drawn, key, least, top_value):
    longest = drawn.shape.index(max(drawn.shape))
    spots = []
    for shift in (0, 1):
        where = [jax.random.randint(jax.random.fold_in(key, axis), (), 0, length) for axis, length in enumerate(drawn.shape)]
        where[longest] = (where[longest] + shift) % drawn.shape[longest]
        spots.append(tuple(where))
    return drawn.at[spots[0]].set(least).at[spots[1]].set(top_value)


def levels(rng, extent, pieces, least, high):
    gain = 1.0
    for position, blocks in pieces:
        steps = jax.random.uniform(jax.random.fold_in(jax.random.fold_in(rng, 6), position), (blocks,), jnp.float32, least / len(pieces), high / len(pieces))
        gain = gain * jnp.repeat(jnp.exp(steps), extent[position] // blocks).reshape((-1,) + (1,) * (len(extent) - 1 - position))
    return gain


def centred(stream_key, dims, scale, limit, pieces=(), kind=jnp.bfloat16):
    values = jax.random.normal(stream_key, dims, jnp.float32) * scale
    if len(pieces) > 0:
        values = levels(stream_key, dims, pieces, -0.22, 0.18) * values
    return jnp.clip(values, min=-limit, max=limit).astype(kind)


def setup_inputs(seed: int = 0, part: int = 0) -> dict:
    arg_keys = jax.random.split(jax.random.key(seed), 9)
    own_keys = jax.random.split(jax.random.fold_in(arg_keys[8], part), 9)
    return {
        "trial": draw_trial(jax.random.fold_in(jax.random.fold_in(arg_keys[8], part), 71), part),
        "loads": centred(arg_keys[1], (NLOAD, ROWS_ALL), 1.0, 6.0, ((1, 16),), jnp.float32),
        "band": centred(arg_keys[2], (BAND, ROWS_ALL), 0.5, 3.0, ((1, 16),), jnp.float32),
        "seeds": set_ends(jax.random.randint(own_keys[3], (SNAP,), 0, NLOAD), jax.random.fold_in(own_keys[3], 1), 0, NLOAD - 1).astype(jnp.int32),
        "iface_rows": draw_iface_rows(jax.random.fold_in(arg_keys[8], 71), part),
        "iface_partner": draw_iface_partner(jax.random.fold_in(arg_keys[8], 71), part),
        "patch_device": draw_patch_device(jax.random.fold_in(arg_keys[8], 71), part),
        "iface_weight": jnp.clip(0.5 + 1.0 * jax.random.uniform(arg_keys[7], (SLOTS,), jnp.float32) ** levels(arg_keys[7], (SLOTS,), ((0, 16),), -0.2, 0.2), 0.5, 1.5),
    }


def reference(trial, loads, band, seeds, iface_rows, iface_partner, patch_device, iface_weight):
    half = (BAND - 1) // 2
    blocks = trial.reshape(SNAP, PATCHES, ROWS_DEV)
    padded = jnp.pad(blocks, ((0, 0), (0, 0), (half, half)))
    coeffs = band.reshape(BAND, PATCHES, ROWS_DEV)
    banded = jnp.zeros((SNAP, PATCHES, ROWS_DEV), jnp.float32)
    for shift_k in range(BAND):
        banded = banded + coeffs[shift_k][None] * padded[:, :, shift_k:shift_k + ROWS_DEV]
    banded = banded.reshape(SNAP, ROWS_ALL)
    slot_ids = jnp.arange(SLOTS, dtype=jnp.int32)
    place = slot_ids // IFACE * ROWS_DEV + iface_rows
    other = patch_device[iface_partner // IFACE] * IFACE + iface_partner % IFACE
    values = trial[:, place]
    coupled = values[:, other] * iface_weight[None, :]
    snapshots = loads[seeds] - banded
    snapshots = snapshots.at[:, place].add(coupled)
    gram = jnp.dot(snapshots.astype(jnp.float32), snapshots.T.astype(jnp.float32), preferred_element_type=jnp.float32, precision=lax.Precision.HIGHEST)
    lower = jnp.linalg.cholesky(gram)
    scale = jnp.sqrt(jnp.float32(ROWS_ALL))
    basis = lax.linalg.triangular_solve(lower, snapshots, left_side=True, lower=True) * scale
    return (lower.T / scale, basis)
```

```python
import functools
import math

import jax
import jax.numpy as jnp
from jax import lax
from jax.experimental import pallas as pl
from jax.experimental.pallas import tpu as pltpu
from jax.sharding import PartitionSpec as P

LANES = 128
F32 = jnp.float32
BF16 = jnp.bfloat16
VMEM_BYTES = 48 * 1024 * 1024


def halves(x):
    high = x.astype(BF16)
    return high, (x - high.astype(F32)).astype(BF16)


def thirds(x):
    high, rest = x.astype(BF16), None
    rest = x - high.astype(F32)
    mid = rest.astype(BF16)
    return high, mid, (rest - mid.astype(F32)).astype(BF16)


def nt_dot(a, b, precision=None):
    return lax.dot_general(
        a, b, (((1,), (1,)), ((), ())), preferred_element_type=F32, precision=precision
    )


def iota(shape, dim):
    return lax.broadcasted_iota(jnp.int32, shape, dim)


def as_column(row):
    count = row.shape[1]
    wide = jnp.broadcast_to(row.astype(F32), (count, count))
    kept = jnp.where(iota((count, count), 0) == iota((count, count), 1), wide, 0.0)
    return jnp.sum(kept, axis=1, keepdims=True).astype(jnp.int32)


def assemble_kernel(
    n, chunk,
    trial_hbm, loads_hbm, band_hbm, seeds_ref, rows_ref, partner_ref, weight_ref,
    parts_hbm, gram_ref,
    trial_v, loads_v, band_v, snap_v, parts_v, hits_v, own_v, near_v, grams_v,
    in_sem, near_send, near_recv, gram_send, gram_recv, out_sem,
):
    me = lax.axis_index("patch")
    right, left = lax.rem(me + 1, n), lax.rem(me + n - 1, n)
    snaps, count = snap_v.shape
    slots = own_v.shape[1]
    width = band_hbm.shape[0]
    half = (width - 1) // 2
    chunks = count // chunk

    barrier = pltpu.get_barrier_semaphore()

    def greet(d, _):
        pl.semaphore_signal(barrier, inc=1, device_id={"patch": lax.rem(me + d, n)},
                            device_id_type=pl.DeviceIdType.MESH)
        return 0

    get_trial = pltpu.make_async_copy(
        trial_hbm, trial_v.at[:, pl.ds(LANES, count)], in_sem.at[0])
    get_loads = pltpu.make_async_copy(loads_hbm, loads_v, in_sem.at[1])
    get_band = pltpu.make_async_copy(band_hbm, band_v, in_sem.at[2])
    get_trial.start()
    get_loads.start()
    get_band.start()
    lax.fori_loop(1, n, greet, 0)
    trial_v[:, :LANES] = jnp.zeros((snaps, LANES), F32)
    trial_v[:, count + LANES:] = jnp.zeros((snaps, LANES), F32)

    rows_col = as_column(rows_ref[...])

    def mark(c, _):
        at = pl.multiple_of(c * chunk, chunk)
        hit = jnp.where(iota((slots, chunk), 1) == rows_col - at, 1.0, 0.0)
        hits_v[:, pl.ds(at, chunk)] = hit.astype(BF16)
        return 0

    def pick(c, own):
        at = pl.multiple_of(c * chunk, chunk)
        both = jnp.concatenate(halves(trial_v[:, pl.ds(at + LANES, chunk)]), axis=0)
        return own + nt_dot(both, hits_v[:, pl.ds(at, chunk)])

    lax.fori_loop(0, chunks, mark, 0)
    get_trial.wait()
    own = lax.fori_loop(0, chunks, pick, jnp.zeros((2 * snaps, slots), F32))
    own_v[...] = own[:snaps] + own[snaps:]
    pl.semaphore_wait(barrier, n - 1)

    def to_near(side, target):
        return pltpu.make_async_remote_copy(
            src_ref=own_v, dst_ref=near_v.at[side], send_sem=near_send.at[side],
            recv_sem=near_recv.at[side], device_id={"patch": target},
            device_id_type=pl.DeviceIdType.MESH)

    to_right, to_left = to_near(0, right), to_near(1, left)
    to_right.start()
    to_left.start()

    get_loads.wait()
    get_band.wait()
    seeds_col = as_column(seeds_ref[...])
    pattern = iota((snaps, 32), 1)
    chooser = jnp.where(
        ((pattern & 7) == seeds_col) & (pattern < 24), 1.0, 0.0).astype(BF16)

    def build(c, gram):
        at = pl.multiple_of(c * chunk, chunk)
        high, mid, low = thirds(loads_v[:, pl.ds(at, chunk)])
        stacked = jnp.concatenate(
            [high.astype(F32), mid.astype(F32), low.astype(F32), jnp.zeros((8, chunk), F32)], axis=0
        ).astype(BF16)
        chosen = jnp.dot(chooser, stacked, preferred_element_type=F32)
        for g in range(snaps // 8):
            wide = trial_v[g * 8:g * 8 + 8, pl.ds(at, chunk + 2 * LANES)]
            acc = chosen[g * 8:g * 8 + 8]
            for k in range(width):
                shift = (half - k) % (chunk + 2 * LANES)
                moved = pltpu.roll(wide, shift, 1) if shift else wide
                acc = acc - band_v[k:k + 1, pl.ds(at, chunk)] * moved[:, LANES:LANES + chunk]
            snap_v[g * 8:g * 8 + 8, pl.ds(at, chunk)] = acc
        both = jnp.concatenate(halves(snap_v[:, pl.ds(at, chunk)]), axis=0)
        right_side = jnp.concatenate([hits_v[:, pl.ds(at, chunk)], both], axis=0)
        return gram + nt_dot(both, right_side)

    gram = lax.fori_loop(0, chunks, build, jnp.zeros((2 * snaps, slots + 2 * snaps), F32))
    gram = gram[:snaps] + gram[snaps:]
    before = gram[:, :slots]
    gram = gram[:, slots:slots + snaps] + gram[:, slots + snaps:]

    shift_to = jnp.where(
        iota((slots, slots), 0) == jnp.broadcast_to(
            partner_ref[...] & (slots - 1), (slots, slots)), 1.0, 0.0).astype(BF16)
    to_right.wait()
    to_left.wait()
    shared = jnp.where(iota((snaps, slots), 1) < slots // 2, near_v[0], near_v[1])
    sorted_ = jnp.dot(jnp.concatenate(thirds(shared), axis=0), shift_to,
                      preferred_element_type=F32)
    coupled = (sorted_[:snaps] + sorted_[snaps:2 * snaps] + sorted_[2 * snaps:]) * weight_ref[...]
    gram = gram + nt_dot(
        jnp.concatenate([coupled, before], axis=1),
        jnp.concatenate([before + coupled, coupled], axis=1),
        precision=lax.Precision.HIGHEST)

    grams_v[me] = jnp.concatenate([gram[i * 8:i * 8 + 8] for i in range(snaps // 8)], axis=1)

    def to_peer(d):
        return pltpu.make_async_remote_copy(
            src_ref=grams_v.at[me], dst_ref=grams_v.at[me], send_sem=gram_send.at[d],
            recv_sem=gram_recv.at[me], device_id={"patch": lax.rem(me + d, n)},
            device_id_type=pl.DeviceIdType.MESH)

    def from_peer(d):
        peer = lax.rem(me + d, n)
        return pltpu.make_async_remote_copy(
            src_ref=grams_v.at[peer], dst_ref=grams_v.at[peer], send_sem=gram_send.at[d],
            recv_sem=gram_recv.at[peer], device_id={"patch": peer},
            device_id_type=pl.DeviceIdType.MESH)

    def send(d, _):
        to_peer(d).start()
        return 0

    lax.fori_loop(1, n, send, 0)

    coupled_parts = jnp.concatenate(halves(coupled), axis=0)

    def finish(c, _):
        at = pl.multiple_of(c * chunk, chunk)
        added = jnp.dot(coupled_parts, hits_v[:, pl.ds(at, chunk)], preferred_element_type=F32)
        whole = snap_v[:, pl.ds(at, chunk)] + (added[:snaps] + added[snaps:])
        parts_v[:, pl.ds(at, chunk)] = jnp.concatenate(halves(whole), axis=0)
        return 0

    lax.fori_loop(0, chunks, finish, 0)
    put = pltpu.make_async_copy(parts_v, parts_hbm, out_sem)
    put.start()

    def arrive(d, _):
        from_peer(d).wait_recv()
        return 0

    lax.fori_loop(1, n, arrive, 0)
    gram_ref[...] = lax.fori_loop(
        0, n, lambda i, t: t + grams_v[i], jnp.zeros(gram_ref.shape, F32))

    def sent(d, _):
        to_peer(d).wait_send()
        return 0

    lax.fori_loop(1, n, sent, 0)
    put.wait()


def basis_kernel(scale, chunk, gram_ref, parts_hbm, factor_ref, basis_hbm,
                 parts_v, basis_v, in_sem, out_sem):
    snaps, count = basis_v.shape
    get = pltpu.make_async_copy(parts_hbm, parts_v, in_sem)
    get.start()
    packed = gram_ref[...]
    gram = jnp.concatenate(
        [packed[:, i * snaps:(i + 1) * snaps] for i in range(snaps // 8)], axis=0)
    line, lane = iota((snaps, 2 * snaps), 0), iota((snaps, 2 * snaps), 1)
    eye = jnp.where(iota((snaps, snaps), 0) == iota((snaps, snaps), 1), 1.0, 0.0)
    work = jnp.concatenate([gram, eye], axis=1)
    for k in range(snaps - 1):
        column = jnp.broadcast_to(work[:, k:k + 1], work.shape)
        pivot = column[k:k + 1]
        row = work[k:k + 1] / pivot
        work = work - jnp.where(line > k, column, 0.0) * row
    pivots = jnp.sum(jnp.where(line == lane, work, 0.0), axis=1, keepdims=True)
    work = work * lax.rsqrt(pivots)
    upper = jnp.where(lane >= line, work, 0.0)
    factor_ref[...] = upper[:, :snaps] * (1.0 / scale)
    high, mid = halves(work[:, snaps:] * scale)
    high, mid = high.astype(F32), mid.astype(F32)
    inverse = jnp.concatenate(
        [jnp.concatenate([high, high], axis=1), jnp.concatenate([mid, mid], axis=1)], axis=0
    ).astype(BF16)
    get.wait()

    def put(c):
        at = pl.ds(pl.multiple_of(c * chunk, chunk), chunk)
        return pltpu.make_async_copy(basis_v.at[:, at], basis_hbm.at[:, at], out_sem.at[c])

    def step(c, _):
        at = pl.ds(pl.multiple_of(c * chunk, chunk), chunk)
        product = jnp.dot(inverse, parts_v[:, at], preferred_element_type=F32)
        basis_v[:, at] = product[:snaps] + product[snaps:]
        put(c).start()
        return 0

    def done(c, _):
        put(c).wait()
        return 0

    lax.fori_loop(0, count // chunk, step, 0)
    lax.fori_loop(0, count // chunk, done, 0)


def per_device(n, trial, loads, band, seeds, iface_rows, iface_partner, patch_device, iface_weight):
    snaps, count = trial.shape
    slots = iface_rows.shape[0]
    width = band.shape[0]
    chunk = 1024
    any_space = pl.BlockSpec(memory_space=pl.ANY)
    vmem = pl.BlockSpec(memory_space=pltpu.VMEM)
    dma = pltpu.SemaphoreType.DMA
    parts, gram = pl.pallas_call(
        functools.partial(assemble_kernel, n, chunk),
        out_shape=(
            jax.ShapeDtypeStruct((2 * snaps, count), BF16),
            jax.ShapeDtypeStruct((8, LANES), F32),
        ),
        in_specs=[any_space, any_space, any_space, vmem, vmem, vmem, vmem],
        out_specs=(any_space, vmem),
        scratch_shapes=[
            pltpu.VMEM((snaps, count + 2 * LANES), F32),
            pltpu.VMEM(loads.shape, F32),
            pltpu.VMEM(band.shape, F32),
            pltpu.VMEM((snaps, count), F32),
            pltpu.VMEM((2 * snaps, count), BF16),
            pltpu.VMEM((slots, count), BF16),
            pltpu.VMEM((snaps, slots), F32),
            pltpu.VMEM((2, snaps, slots), F32),
            pltpu.VMEM((n, 8, LANES), F32),
            dma((3,)), dma((2,)), dma((2,)), dma((n,)), dma((n,)), dma,
        ],
        compiler_params=pltpu.CompilerParams(
            collective_id=0, has_side_effects=True, vmem_limit_bytes=VMEM_BYTES),
        name="assemble",
    )(trial, loads, band, seeds.reshape(1, snaps), iface_rows.reshape(1, slots),
      iface_partner.reshape(1, slots), iface_weight.reshape(1, slots))
    out_chunk = 2048
    scale = math.sqrt(count * n)
    factor, basis = pl.pallas_call(
        functools.partial(basis_kernel, scale, out_chunk),
        out_shape=(
            jax.ShapeDtypeStruct((snaps, snaps), F32),
            jax.ShapeDtypeStruct((snaps, count), F32),
        ),
        in_specs=[vmem, any_space],
        out_specs=(vmem, any_space),
        scratch_shapes=[
            pltpu.VMEM((2 * snaps, count), BF16),
            pltpu.VMEM((snaps, count), F32),
            dma, dma((count // out_chunk,)),
        ],
        compiler_params=pltpu.CompilerParams(vmem_limit_bytes=VMEM_BYTES),
        name="basis",
    )(gram, parts)
    return factor, basis


def solution(mesh):
    placed = (
        P("groups", "patch"),
        P(None, "patch"),
        P(None, "patch"),
        P("groups"),
        P("patch"),
        P("patch"),
        P(),
        P("patch"),
    )
    return jax.shard_map(
        functools.partial(per_device, mesh.shape["patch"]),
        mesh=mesh,
        in_specs=placed,
        out_specs=(P("groups", None), P("groups", "patch")),
        check_vma=False,
    )
```

```python
import functools
import math

import jax
import jax.numpy as jnp
from jax import lax
from jax.experimental import pallas as pl
from jax.experimental.pallas import tpu as pltpu
from jax.sharding import PartitionSpec as P

LANES = 128
F32 = jnp.float32
BF16 = jnp.bfloat16
VMEM_BYTES = 60 * 1024 * 1024


def halves(x):
    high = x.astype(BF16)
    return high, (x - high.astype(F32)).astype(BF16)


def thirds(x):
    high, rest = x.astype(BF16), None
    rest = x - high.astype(F32)
    mid = rest.astype(BF16)
    return high, mid, (rest - mid.astype(F32)).astype(BF16)


def nt_dot(a, b, precision=None):
    return lax.dot_general(
        a, b, (((1,), (1,)), ((), ())), preferred_element_type=F32, precision=precision
    )


def iota(shape, dim):
    return lax.broadcasted_iota(jnp.int32, shape, dim)


def as_column(row):
    count = row.shape[1]
    wide = jnp.broadcast_to(row.astype(F32), (count, count))
    kept = jnp.where(iota((count, count), 0) == iota((count, count), 1), wide, 0.0)
    return jnp.sum(kept, axis=1, keepdims=True).astype(jnp.int32)


def assemble_kernel(
    n, chunk, pieces,
    trial_hbm, loads_hbm, band_hbm, seeds_hbm, rows_hbm, partner_hbm, weight_hbm,
    parts_hbm, gram_ref,
    trial_v, loads_v, band_v, turned_v, snap_v, parts_v, seeds_v, rows_v, partner_v, weight_v,
    own_v, near_v, grams_v,
    in_sem, near_send, near_recv, gram_send, gram_recv, out_sem,
):
    me = lax.axis_index("patch")
    right, left = lax.rem(me + 1, n), lax.rem(me + n - 1, n)
    snaps, count = snap_v.shape
    slots = own_v.shape[1]
    width = band_hbm.shape[0]
    piece = count // pieces
    wide_count = count + 2 * LANES

    barrier = pltpu.get_barrier_semaphore()

    def greet(d, _):
        pl.semaphore_signal(barrier, inc=1, device_id={"patch": lax.rem(me + d, n)},
                            device_id_type=pl.DeviceIdType.MESH)
        return 0

    inside = pl.ds(LANES, count)
    get_rows = pltpu.make_async_copy(rows_hbm, rows_v, in_sem.at[0])
    get_band = pltpu.make_async_copy(band_hbm, band_v.at[:, inside], in_sem.at[1])
    get_loads = pltpu.make_async_copy(loads_hbm, loads_v, in_sem.at[2])
    get_seeds = pltpu.make_async_copy(seeds_hbm, seeds_v, in_sem.at[3])
    get_partner = pltpu.make_async_copy(partner_hbm, partner_v, in_sem.at[4])
    get_weight = pltpu.make_async_copy(weight_hbm, weight_v, in_sem.at[5])
    get_trial = [
        pltpu.make_async_copy(
            trial_hbm.at[:, pl.ds(p * piece, piece)],
            trial_v.at[:, pl.ds(LANES + p * piece, piece)], in_sem.at[6 + p])
        for p in range(pieces)
    ]
    for copy in [get_rows, get_band] + get_trial + [get_loads, get_seeds, get_partner, get_weight]:
        copy.start()
    lax.fori_loop(1, n, greet, 0)
    for edge in (0, count + LANES):
        trial_v[:, edge:edge + LANES] = jnp.zeros((snaps, LANES), F32)
        band_v[:, edge:edge + LANES] = jnp.zeros((width, LANES), F32)

    get_rows.wait()
    get_band.wait()
    first = band_v[0:8, :]
    line = iota((8, wide_count), 0)
    turned_v[0:8, :] = jnp.where(
        line < 3, pltpu.roll(first, wide_count - 3, 1),
        jnp.where(line < 6, first, pltpu.roll(first, 3, 1)))
    turned_v[8:9, :] = pltpu.roll(band_v[8:9, :], 3, 1)

    rows = rows_v[...]

    def hits(at, size):
        return jnp.where(iota((size, slots), 0) == rows - at, 1.0, 0.0).astype(BF16)

    own = jnp.zeros((2 * snaps, slots), F32)
    for p in range(pieces):
        get_trial[p].wait()
        both = jnp.concatenate(
            halves(trial_v[:, LANES + p * piece:LANES + (p + 1) * piece]), axis=0)
        own = own + jnp.dot(both, hits(p * piece, piece), preferred_element_type=F32)
    own_v[...] = own[:snaps] + own[snaps:]
    pl.semaphore_wait(barrier, n - 1)

    def to_near(side, target):
        return pltpu.make_async_remote_copy(
            src_ref=own_v, dst_ref=near_v.at[side], send_sem=near_send.at[side],
            recv_sem=near_recv.at[side], device_id={"patch": target},
            device_id_type=pl.DeviceIdType.MESH)

    to_right, to_left = to_near(0, right), to_near(1, left)
    to_right.start()
    to_left.start()

    for copy in (get_loads, get_seeds, get_partner, get_weight):
        copy.wait()
    seeds_col = as_column(seeds_v[...])
    pattern = iota((snaps, 32), 1)
    chooser = jnp.where(
        ((pattern & 7) == seeds_col) & (pattern < 24), 1.0, 0.0).astype(BF16)

    span = chunk + 2 * LANES
    gram = jnp.zeros((2 * snaps, 2 * snaps), F32)
    before = jnp.zeros((2 * snaps, slots), F32)
    for c in range(count // chunk):
        at = c * chunk
        high, mid, low = thirds(loads_v[:, at:at + chunk])
        stacked = jnp.concatenate(
            [high.astype(F32), mid.astype(F32), low.astype(F32), jnp.zeros((8, chunk), F32)], axis=0
        ).astype(BF16)
        chosen = jnp.dot(chooser, stacked, preferred_element_type=F32)
        for g in range(snaps // 8):
            here = trial_v[g * 8:g * 8 + 8, at:at + span]
            behind, ahead = pltpu.roll(here, 1, 1), pltpu.roll(here, span - 1, 1)
            acc = chosen[g * 8:g * 8 + 8]
            for far in (-1, 0, 1):
                k = 3 * far + 4
                term = (turned_v[k - 1:k, at:at + span] * behind
                        + turned_v[k:k + 1, at:at + span] * here
                        + turned_v[k + 1:k + 2, at:at + span] * ahead)
                if far:
                    term = pltpu.roll(term, (-3 * far) % span, 1)
                acc = acc - term[:, LANES:LANES + chunk]
            snap_v[g * 8:g * 8 + 8, at:at + chunk] = acc
        both = jnp.concatenate(halves(snap_v[:, at:at + chunk]), axis=0)
        gram = gram + nt_dot(both, both)
        before = before + jnp.dot(both, hits(at, chunk), preferred_element_type=F32)
    gram = gram[:snaps] + gram[snaps:]
    gram = gram[:, :snaps] + gram[:, snaps:]
    before = before[:snaps] + before[snaps:]

    order = jnp.where(
        iota((slots, slots), 0) == (partner_v[...] & (slots - 1)), 1.0, 0.0).astype(BF16)
    to_right.wait()
    to_left.wait()
    shared = jnp.where(iota((snaps, slots), 1) < slots // 2, near_v[0], near_v[1])
    coupled = jnp.dot(jnp.concatenate(thirds(shared), axis=0), order, preferred_element_type=F32)
    coupled = (coupled[:snaps] + coupled[snaps:2 * snaps] + coupled[2 * snaps:]) * weight_v[...]
    gram = gram + nt_dot(
        jnp.concatenate([coupled, before], axis=1),
        jnp.concatenate([before + coupled, coupled], axis=1),
        precision=lax.Precision.HIGHEST)

    grams_v[me] = jnp.concatenate([gram[i * 8:i * 8 + 8] for i in range(snaps // 8)], axis=1)

    def to_peer(d):
        return pltpu.make_async_remote_copy(
            src_ref=grams_v.at[me], dst_ref=grams_v.at[me], send_sem=gram_send.at[d],
            recv_sem=gram_recv.at[me], device_id={"patch": lax.rem(me + d, n)},
            device_id_type=pl.DeviceIdType.MESH)

    def from_peer(d):
        peer = lax.rem(me + d, n)
        return pltpu.make_async_remote_copy(
            src_ref=grams_v.at[peer], dst_ref=grams_v.at[peer], send_sem=gram_send.at[d],
            recv_sem=gram_recv.at[peer], device_id={"patch": peer},
            device_id_type=pl.DeviceIdType.MESH)

    def send(d, _):
        to_peer(d).start()
        return 0

    lax.fori_loop(1, n, send, 0)

    rows_col = as_column(rows)
    coupled_parts = jnp.concatenate(halves(coupled), axis=0)
    puts = []
    for p in range(pieces):
        at = p * piece
        hit = jnp.where(iota((slots, piece), 1) == rows_col - at, 1.0, 0.0).astype(BF16)
        added = jnp.dot(coupled_parts, hit, preferred_element_type=F32)
        whole = snap_v[:, at:at + piece] + (added[:snaps] + added[snaps:])
        parts_v[:, at:at + piece] = jnp.concatenate(halves(whole), axis=0)
        cut = pl.ds(at, piece)
        puts.append(pltpu.make_async_copy(parts_v.at[:, cut], parts_hbm.at[:, cut], out_sem.at[p]))
        puts[p].start()

    def arrive(d, _):
        from_peer(d).wait_recv()
        return 0

    lax.fori_loop(1, n, arrive, 0)
    gram_ref[...] = lax.fori_loop(
        0, n, lambda i, t: t + grams_v[i], jnp.zeros(gram_ref.shape, F32))

    def sent(d, _):
        to_peer(d).wait_send()
        return 0

    lax.fori_loop(1, n, sent, 0)
    for put in puts:
        put.wait()


def basis_kernel(scale, chunk, gram_ref, parts_hbm, factor_ref, basis_hbm,
                 parts_v, basis_v, in_sem, out_sem):
    snaps, count = basis_v.shape
    get = pltpu.make_async_copy(parts_hbm, parts_v, in_sem)
    get.start()
    packed = gram_ref[...]
    gram = jnp.concatenate(
        [packed[:, i * snaps:(i + 1) * snaps] for i in range(snaps // 8)], axis=0)
    line, lane = iota((snaps, 2 * snaps), 0), iota((snaps, 2 * snaps), 1)
    eye = jnp.where(iota((snaps, snaps), 0) == iota((snaps, snaps), 1), 1.0, 0.0)
    work = jnp.concatenate([gram, eye], axis=1)
    for k in range(0, snaps, 2):
        column0 = jnp.broadcast_to(work[:, k:k + 1], work.shape)
        column1 = jnp.broadcast_to(work[:, k + 1:k + 2], work.shape)
        row0 = work[k:k + 1]
        inverse0 = 1.0 / column0[k:k + 1]
        share = column0[k + 1:k + 2] * inverse0
        row1 = work[k + 1:k + 2] - share * row0
        inverse1 = 1.0 / (column1[k + 1:k + 2] - share * column1[k:k + 1])
        column1 = column1 - column0 * (column1[k:k + 1] * inverse0)
        work = (work - jnp.where(line > k, column0, 0.0) * (row0 * inverse0)
                - jnp.where(line > k + 1, column1, 0.0) * (row1 * inverse1))
    pivots = jnp.sum(jnp.where(line == lane, work, 0.0), axis=1, keepdims=True)
    work = work * lax.rsqrt(pivots)
    upper = jnp.where(lane >= line, work, 0.0)
    factor_ref[...] = upper[:, :snaps] * (1.0 / scale)
    high, mid = halves(work[:, snaps:] * scale)
    high, mid = high.astype(F32), mid.astype(F32)
    inverse = jnp.concatenate(
        [jnp.concatenate([high, high], axis=1), jnp.concatenate([mid, mid], axis=1)], axis=0
    ).astype(BF16)
    get.wait()
    puts = []
    for c in range(count // chunk):
        at = pl.ds(c * chunk, chunk)
        product = jnp.dot(inverse, parts_v[:, at], preferred_element_type=F32)
        basis_v[:, at] = product[:snaps] + product[snaps:]
        puts.append(pltpu.make_async_copy(basis_v.at[:, at], basis_hbm.at[:, at], out_sem.at[c]))
        puts[c].start()
    for put in puts:
        put.wait()


def per_device(n, trial, loads, band, seeds, iface_rows, iface_partner, patch_device, iface_weight):
    snaps, count = trial.shape
    slots = iface_rows.shape[0]
    width = band.shape[0]
    chunk, pieces, out_chunk = 1024, 4, 4096
    hbm = pl.BlockSpec(memory_space=pltpu.HBM)
    vmem = pl.BlockSpec(memory_space=pltpu.VMEM)
    dma = pltpu.SemaphoreType.DMA
    parts, gram = pl.pallas_call(
        functools.partial(assemble_kernel, n, chunk, pieces),
        out_shape=(
            jax.ShapeDtypeStruct((2 * snaps, count), BF16),
            jax.ShapeDtypeStruct((8, LANES), F32),
        ),
        in_specs=[hbm] * 7,
        out_specs=(hbm, vmem),
        scratch_shapes=[
            pltpu.VMEM((snaps, count + 2 * LANES), F32),
            pltpu.VMEM(loads.shape, F32),
            pltpu.VMEM((width, count + 2 * LANES), F32),
            pltpu.VMEM((width, count + 2 * LANES), F32),
            pltpu.VMEM((snaps, count), F32),
            pltpu.VMEM((2 * snaps, count), BF16),
            pltpu.VMEM((1, snaps), jnp.int32),
            pltpu.VMEM((1, slots), jnp.int32),
            pltpu.VMEM((1, slots), jnp.int32),
            pltpu.VMEM((1, slots), F32),
            pltpu.VMEM((snaps, slots), F32),
            pltpu.VMEM((2, snaps, slots), F32),
            pltpu.VMEM((n, 8, LANES), F32),
            dma((6 + pieces,)), dma((2,)), dma((2,)), dma((n,)), dma((n,)),
            dma((pieces,)),
        ],
        compiler_params=pltpu.CompilerParams(
            collective_id=0, has_side_effects=True, vmem_limit_bytes=VMEM_BYTES),
        name="assemble",
    )(trial, loads, band, seeds.reshape(1, snaps), iface_rows.reshape(1, slots),
      iface_partner.reshape(1, slots), iface_weight.reshape(1, slots))
    scale = math.sqrt(count * n)
    factor, basis = pl.pallas_call(
        functools.partial(basis_kernel, scale, out_chunk),
        out_shape=(
            jax.ShapeDtypeStruct((snaps, snaps), F32),
            jax.ShapeDtypeStruct((snaps, count), F32),
        ),
        in_specs=[vmem, hbm],
        out_specs=(vmem, hbm),
        scratch_shapes=[
            pltpu.VMEM((2 * snaps, count), BF16),
            pltpu.VMEM((snaps, count), F32),
            dma, dma((count // out_chunk,)),
        ],
        compiler_params=pltpu.CompilerParams(vmem_limit_bytes=VMEM_BYTES),
        name="basis",
    )(gram, parts)
    return factor, basis


def solution(mesh):
    placed = (
        P("groups", "patch"),
        P(None, "patch"),
        P(None, "patch"),
        P("groups"),
        P("patch"),
        P("patch"),
        P(),
        P("patch"),
    )
    return jax.shard_map(
        functools.partial(per_device, mesh.shape["patch"]),
        mesh=mesh,
        in_specs=placed,
        out_specs=(P("groups", None), P("groups", "patch")),
        check_vma=False,
    )
```

```python
import functools
import math

import jax
import jax.numpy as jnp
from jax import lax
from jax.experimental import pallas as pl
from jax.experimental.pallas import tpu as pltpu
from jax.sharding import PartitionSpec as P

LANES = 128
F32 = jnp.float32
BF16 = jnp.bfloat16
VMEM_BYTES = 60 * 1024 * 1024


def halves(x):
    high = x.astype(BF16)
    return high, (x - high.astype(F32)).astype(BF16)


def thirds(x):
    high, rest = x.astype(BF16), None
    rest = x - high.astype(F32)
    mid = rest.astype(BF16)
    return high, mid, (rest - mid.astype(F32)).astype(BF16)


def nt_dot(a, b, precision=None):
    return lax.dot_general(
        a, b, (((1,), (1,)), ((), ())), preferred_element_type=F32, precision=precision
    )


def iota(shape, dim):
    return lax.broadcasted_iota(jnp.int32, shape, dim)


def as_column(row):
    count = row.shape[1]
    wide = jnp.broadcast_to(row.astype(F32), (count, count))
    kept = jnp.where(iota((count, count), 0) == iota((count, count), 1), wide, 0.0)
    return jnp.sum(kept, axis=1, keepdims=True).astype(jnp.int32)


def assemble_kernel(
    n, chunk, pieces,
    trial_hbm, loads_hbm, band_hbm, seeds_hbm, rows_hbm, partner_hbm, weight_hbm,
    parts_hbm, gram_ref,
    trial_v, loads_v, band_v, turned_v, snap_v, parts_v, seeds_v, rows_v, partner_v, weight_v,
    own_v, near_v, grams_v,
    in_sem, near_send, near_recv, gram_send, gram_recv, out_sem,
):
    me = lax.axis_index("patch")
    right, left = lax.rem(me + 1, n), lax.rem(me + n - 1, n)
    snaps, count = snap_v.shape
    slots = own_v.shape[1]
    width = band_hbm.shape[0]
    piece = count // pieces
    wide_count = count + 2 * LANES

    barrier = pltpu.get_barrier_semaphore()

    def greet(d, _):
        pl.semaphore_signal(barrier, inc=1, device_id={"patch": lax.rem(me + d, n)},
                            device_id_type=pl.DeviceIdType.MESH)
        return 0

    inside = pl.ds(LANES, count)
    get_rows = pltpu.make_async_copy(rows_hbm, rows_v, in_sem.at[0])
    get_band = pltpu.make_async_copy(band_hbm, band_v.at[:, inside], in_sem.at[1])
    get_loads = pltpu.make_async_copy(loads_hbm, loads_v, in_sem.at[2])
    get_seeds = pltpu.make_async_copy(seeds_hbm, seeds_v, in_sem.at[3])
    get_partner = pltpu.make_async_copy(partner_hbm, partner_v, in_sem.at[4])
    get_weight = pltpu.make_async_copy(weight_hbm, weight_v, in_sem.at[5])
    get_trial = [
        pltpu.make_async_copy(
            trial_hbm.at[:, pl.ds(p * piece, piece)],
            trial_v.at[:, pl.ds(LANES + p * piece, piece)], in_sem.at[6 + p])
        for p in range(pieces)
    ]
    for copy in [get_rows, get_band] + get_trial + [get_loads, get_seeds, get_partner, get_weight]:
        copy.start()
    lax.fori_loop(1, n, greet, 0)
    for edge in (0, count + LANES):
        trial_v[:, edge:edge + LANES] = jnp.zeros((snaps, LANES), F32)
        band_v[:, edge:edge + LANES] = jnp.zeros((width, LANES), F32)

    get_rows.wait()
    get_band.wait()
    first = band_v[0:8, :]
    line = iota((8, wide_count), 0)
    turned_v[0:8, :] = jnp.where(
        line < 3, pltpu.roll(first, wide_count - 3, 1),
        jnp.where(line < 6, first, pltpu.roll(first, 3, 1)))
    turned_v[8:9, :] = pltpu.roll(band_v[8:9, :], 3, 1)

    rows = rows_v[...]

    def hits(at, size):
        return jnp.where(iota((size, slots), 0) == rows - at, 1.0, 0.0).astype(BF16)

    own = jnp.zeros((2 * snaps, slots), F32)
    for p in range(pieces):
        get_trial[p].wait()
        both = jnp.concatenate(
            halves(trial_v[:, LANES + p * piece:LANES + (p + 1) * piece]), axis=0)
        own = own + jnp.dot(both, hits(p * piece, piece), preferred_element_type=F32)
    own_v[...] = own[:snaps] + own[snaps:]
    pl.semaphore_wait(barrier, n - 1)

    def to_near(side, target):
        return pltpu.make_async_remote_copy(
            src_ref=own_v, dst_ref=near_v.at[side], send_sem=near_send.at[side],
            recv_sem=near_recv.at[side], device_id={"patch": target},
            device_id_type=pl.DeviceIdType.MESH)

    to_right, to_left = to_near(0, right), to_near(1, left)
    to_right.start()
    to_left.start()

    for copy in (get_loads, get_seeds, get_partner, get_weight):
        copy.wait()
    seeds_col = as_column(seeds_v[...])
    pattern = iota((snaps, 32), 1)
    chooser = jnp.where(
        ((pattern & 7) == seeds_col) & (pattern < 24), 1.0, 0.0).astype(BF16)

    span = chunk + 2 * LANES
    gram = jnp.zeros((2 * snaps, 2 * snaps), F32)
    before = jnp.zeros((2 * snaps, slots), F32)
    for c in range(count // chunk):
        at = c * chunk
        high, mid, low = thirds(loads_v[:, at:at + chunk])
        stacked = jnp.concatenate(
            [high.astype(F32), mid.astype(F32), low.astype(F32), jnp.zeros((8, chunk), F32)], axis=0
        ).astype(BF16)
        chosen = jnp.dot(chooser, stacked, preferred_element_type=F32)
        for g in range(snaps // 8):
            here = trial_v[g * 8:g * 8 + 8, at:at + span]
            behind, ahead = pltpu.roll(here, 1, 1), pltpu.roll(here, span - 1, 1)
            acc = chosen[g * 8:g * 8 + 8]
            for far in (-1, 0, 1):
                k = 3 * far + 4
                term = (turned_v[k - 1:k, at:at + span] * behind
                        + turned_v[k:k + 1, at:at + span] * here
                        + turned_v[k + 1:k + 2, at:at + span] * ahead)
                if far:
                    term = pltpu.roll(term, (-3 * far) % span, 1)
                acc = acc - term[:, LANES:LANES + chunk]
            snap_v[g * 8:g * 8 + 8, at:at + chunk] = acc
        both = jnp.concatenate(halves(snap_v[:, at:at + chunk]), axis=0)
        gram = gram + nt_dot(both, both)
        before = before + jnp.dot(both, hits(at, chunk), preferred_element_type=F32)
    gram = gram[:snaps] + gram[snaps:]
    gram = gram[:, :snaps] + gram[:, snaps:]
    before = before[:snaps] + before[snaps:]

    order = jnp.where(
        iota((slots, slots), 0) == (partner_v[...] & (slots - 1)), 1.0, 0.0).astype(BF16)
    to_right.wait()
    to_left.wait()
    shared = jnp.where(iota((snaps, slots), 1) < slots // 2, near_v[0], near_v[1])
    coupled = jnp.dot(jnp.concatenate(thirds(shared), axis=0), order, preferred_element_type=F32)
    coupled = (coupled[:snaps] + coupled[snaps:2 * snaps] + coupled[2 * snaps:]) * weight_v[...]
    gram = gram + nt_dot(
        jnp.concatenate([coupled, before], axis=1),
        jnp.concatenate([before + coupled, coupled], axis=1),
        precision=lax.Precision.HIGHEST)

    grams_v[me] = jnp.concatenate([gram[i * 8:i * 8 + 8] for i in range(snaps // 8)], axis=1)

    def to_peer(d):
        return pltpu.make_async_remote_copy(
            src_ref=grams_v.at[me], dst_ref=grams_v.at[me], send_sem=gram_send.at[d],
            recv_sem=gram_recv.at[me], device_id={"patch": lax.rem(me + d, n)},
            device_id_type=pl.DeviceIdType.MESH)

    def from_peer(d):
        peer = lax.rem(me + d, n)
        return pltpu.make_async_remote_copy(
            src_ref=grams_v.at[peer], dst_ref=grams_v.at[peer], send_sem=gram_send.at[d],
            recv_sem=gram_recv.at[peer], device_id={"patch": peer},
            device_id_type=pl.DeviceIdType.MESH)

    def send(d, _):
        to_peer(d).start()
        return 0

    lax.fori_loop(1, n, send, 0)

    rows_col = as_column(rows)
    coupled_parts = jnp.concatenate(halves(coupled), axis=0)
    puts = []
    for p in range(pieces):
        at = p * piece
        hit = jnp.where(iota((slots, piece), 1) == rows_col - at, 1.0, 0.0).astype(BF16)
        added = jnp.dot(coupled_parts, hit, preferred_element_type=F32)
        whole = snap_v[:, at:at + piece] + (added[:snaps] + added[snaps:])
        parts_v[:, at:at + piece] = jnp.concatenate(halves(whole), axis=0)
        cut = pl.ds(at, piece)
        puts.append(pltpu.make_async_copy(parts_v.at[:, cut], parts_hbm.at[:, cut], out_sem.at[p]))
        puts[p].start()

    def arrive(d, _):
        from_peer(d).wait_recv()
        return 0

    lax.fori_loop(1, n, arrive, 0)
    total = grams_v[0]
    for i in range(1, n):
        total = total + grams_v[i]
    gram_ref[...] = total

    def sent(d, _):
        to_peer(d).wait_send()
        return 0

    lax.fori_loop(1, n, sent, 0)
    for put in puts:
        put.wait()


def basis_kernel(scale, chunk, block, gram_ref, parts_hbm, factor_ref, basis_hbm,
                 parts_v, basis_v, in_sem, out_sem):
    snaps, count = basis_v.shape
    get = pltpu.make_async_copy(parts_hbm, parts_v, in_sem)
    get.start()
    packed = gram_ref[...]
    gram = jnp.concatenate(
        [packed[:, i * snaps:(i + 1) * snaps] for i in range(snaps // 8)], axis=0)
    line, lane = iota((snaps, 2 * snaps), 0), iota((snaps, 2 * snaps), 1)
    eye = jnp.where(iota((snaps, snaps), 0) == iota((snaps, snaps), 1), 1.0, 0.0)
    work = jnp.concatenate([gram, eye], axis=1)
    for k in range(0, snaps, block):
        columns = [jnp.broadcast_to(work[:, k + j:k + j + 1], work.shape) for j in range(block)]
        for j in range(block):
            m = k + j
            inverse = 1.0 / columns[j][m:m + 1]
            work = work - jnp.where(line > m, columns[j], 0.0) * (work[m:m + 1] * inverse)
            for i in range(j + 1, block):
                columns[i] = columns[i] - columns[j] * (columns[i][m:m + 1] * inverse)
    pivots = jnp.sum(jnp.where(line == lane, work, 0.0), axis=1, keepdims=True)
    work = work * lax.rsqrt(pivots)
    upper = jnp.where(lane >= line, work, 0.0)
    factor_ref[...] = upper[:, :snaps] * (1.0 / scale)
    high, mid = halves(work[:, snaps:] * scale)
    high, mid = high.astype(F32), mid.astype(F32)
    inverse = jnp.concatenate(
        [jnp.concatenate([high, high], axis=1), jnp.concatenate([mid, mid], axis=1)], axis=0
    ).astype(BF16)
    get.wait()
    puts = []
    for c in range(count // chunk):
        at = pl.ds(c * chunk, chunk)
        product = jnp.dot(inverse, parts_v[:, at], preferred_element_type=F32)
        basis_v[:, at] = product[:snaps] + product[snaps:]
        puts.append(pltpu.make_async_copy(basis_v.at[:, at], basis_hbm.at[:, at], out_sem.at[c]))
        puts[c].start()
    for put in puts:
        put.wait()


def per_device(n, trial, loads, band, seeds, iface_rows, iface_partner, patch_device, iface_weight):
    snaps, count = trial.shape
    slots = iface_rows.shape[0]
    width = band.shape[0]
    chunk, pieces, out_chunk = 1024, 2, 4096
    hbm = pl.BlockSpec(memory_space=pltpu.HBM)
    vmem = pl.BlockSpec(memory_space=pltpu.VMEM)
    dma = pltpu.SemaphoreType.DMA
    parts, gram = pl.pallas_call(
        functools.partial(assemble_kernel, n, chunk, pieces),
        out_shape=(
            jax.ShapeDtypeStruct((2 * snaps, count), BF16),
            jax.ShapeDtypeStruct((8, LANES), F32),
        ),
        in_specs=[hbm] * 7,
        out_specs=(hbm, vmem),
        scratch_shapes=[
            pltpu.VMEM((snaps, count + 2 * LANES), F32),
            pltpu.VMEM(loads.shape, F32),
            pltpu.VMEM((width, count + 2 * LANES), F32),
            pltpu.VMEM((width, count + 2 * LANES), F32),
            pltpu.VMEM((snaps, count), F32),
            pltpu.VMEM((2 * snaps, count), BF16),
            pltpu.VMEM((1, snaps), jnp.int32),
            pltpu.VMEM((1, slots), jnp.int32),
            pltpu.VMEM((1, slots), jnp.int32),
            pltpu.VMEM((1, slots), F32),
            pltpu.VMEM((snaps, slots), F32),
            pltpu.VMEM((2, snaps, slots), F32),
            pltpu.VMEM((n, 8, LANES), F32),
            dma((6 + pieces,)), dma((2,)), dma((2,)), dma((n,)), dma((n,)),
            dma((pieces,)),
        ],
        compiler_params=pltpu.CompilerParams(
            collective_id=0, has_side_effects=True, vmem_limit_bytes=VMEM_BYTES),
        name="assemble",
    )(trial, loads, band, seeds.reshape(1, snaps), iface_rows.reshape(1, slots),
      iface_partner.reshape(1, slots), iface_weight.reshape(1, slots))
    scale = math.sqrt(count * n)
    factor, basis = pl.pallas_call(
        functools.partial(basis_kernel, scale, out_chunk, 16),
        out_shape=(
            jax.ShapeDtypeStruct((snaps, snaps), F32),
            jax.ShapeDtypeStruct((snaps, count), F32),
        ),
        in_specs=[vmem, hbm],
        out_specs=(vmem, hbm),
        scratch_shapes=[
            pltpu.VMEM((2 * snaps, count), BF16),
            pltpu.VMEM((snaps, count), F32),
            dma, dma((count // out_chunk,)),
        ],
        compiler_params=pltpu.CompilerParams(vmem_limit_bytes=VMEM_BYTES),
        name="basis",
    )(gram, parts)
    return factor, basis


def solution(mesh):
    placed = (
        P("groups", "patch"),
        P(None, "patch"),
        P(None, "patch"),
        P("groups"),
        P("patch"),
        P("patch"),
        P(),
        P("patch"),
    )
    return jax.shard_map(
        functools.partial(per_device, mesh.shape["patch"]),
        mesh=mesh,
        in_specs=placed,
        out_specs=(P("groups", None), P("groups", "patch")),
        check_vma=False,
    )
```
